256 devices in a mesh: seq: 64 (over x, y_hi, z), tp: 4 (over y_lo, core).
Axes of the slice: x: 4, y: 4 (y_hi: 2, y_lo: 2; y = y_hi * 2 + y_lo), z: 8, core: 2. Of those that a mesh axis runs over, the one named last changes fastest.
Arguments:
- queries: bfloat16 [8192, 16384], P(('tp', 'seq')), may hold values from -8 to 8
- keys: bfloat16 [8192, 1024], P(('tp', 'seq')), may hold values from -5 to 5
- values: bfloat16 [8192, 1024], P(('tp', 'seq')), may hold values from -6 to 6
- window_lag: int32 [1], replicated, may hold values from 0 to 8191
Outputs:
- attended: bfloat16 [8192, 16384], P(('tp', 'seq'))
The draws below stay inside these ranges and needn't reach their ends.
All inputs are finite; a program needn't handle non-finite values.
Results may differ from the reference program's by a relative error of at most 0.006.
Values may be sent and summed in bfloat16 or wider, within the bound.
No kernel may reach another device: no remote copies, remote signals or barrier semaphores. Data moves between devices by JAX's collectives and lax.ppermute only.
A program may use at most 64 MiB of HBM per device.

```python
import math
import jax
import jax.numpy as jnp
from jax import lax

HQ = 128
KV = 8
HD = 128
TOKENS = 8192


def draw_queries(key, part):
    key = jax.random.fold_in(key, 11)
    base_key = jax.random.fold_in(key, 0)
    drawn_values = 2.5 * jax.random.normal(base_key, (TOKENS, HQ, HD), jnp.float32)
    return jnp.clip(drawn_values, -8.0, 8.0).reshape(TOKENS, HQ * HD).astype(jnp.bfloat16)


def draw_keys(key, part):
    key = jax.random.fold_in(key, 13)
    base_key = jax.random.fold_in(key, 0)
    drawn_values = jax.random.normal(base_key, (TOKENS, KV, HD), jnp.float32)
    return jnp.clip(drawn_values, -5.0, 5.0).reshape(TOKENS, KV * HD).astype(jnp.bfloat16)


def shard_levels(own_key, extent, cuts, low, high):
    gain, own = 1.0, jax.random.fold_in(own_key, 6)
    for dim, blocks in cuts:
        heights = jnp.exp(jax.random.uniform(jax.random.fold_in(own, dim), (blocks,), jnp.float32, low / len(cuts), high / len(cuts)))
        gain = gain * jnp.repeat(heights, extent[dim] // blocks).reshape([-1 if axis == dim else 1 for axis in range(len(extent))])
    return gain


def noise(key, extent, scale, bound, cuts=(), held_as=jnp.bfloat16):
    values = jax.random.normal(key, extent, jnp.float32) * scale
    if len(cuts) > 0:
        values = shard_levels(key, extent, cuts, -0.22, 0.18) * values
    return jnp.clip(values, min=-bound, max=bound).astype(held_as)


def setup_inputs(seed: int = 0) -> dict:
    splits = jax.random.split(jax.random.key(seed), 5)
    return {
        "queries": draw_queries(jax.random.fold_in(splits[4], 71), 0),
        "keys": draw_keys(jax.random.fold_in(splits[4], 71), 0),
        "values": noise(splits[2], (TOKENS, KV * HD), 1.0, 6.0, ((0, 256),)),
        "window_lag": jax.random.randint(splits[3], (1,), 0, TOKENS).astype(jnp.int32),
    }


def reference(queries, keys, values, window_lag):
    length = queries.shape[0]
    group_size = HQ // KV
    score_scale = 1.0 / math.sqrt(HD)
    query_heads = queries.reshape(length, HQ, HD)
    key_heads = keys.reshape(length, KV, HD)
    value_heads = values.reshape(length, KV, HD)
    query_pos = lax.broadcasted_iota(jnp.int32, (length, length), 0)
    key_pos = lax.broadcasted_iota(jnp.int32, (length, length), 1)
    visible = key_pos <= query_pos + window_lag[0]

    def one_head(head):
        query_one = lax.dynamic_index_in_dim(query_heads, head, 1, keepdims=False)
        key_one = lax.dynamic_index_in_dim(key_heads, head // group_size, 1, keepdims=False)
        value_one = lax.dynamic_index_in_dim(value_heads, head // group_size, 1, keepdims=False)
        scores = jnp.dot(query_one, key_one.T, preferred_element_type=jnp.float32) * score_scale
        scores = jnp.where(visible, scores, -jnp.inf)
        peak = lax.optimization_barrier(jnp.max(scores, axis=1, keepdims=True))
        weights = jnp.exp(scores - peak)
        norm_sum = lax.optimization_barrier(jnp.sum(weights, axis=1, keepdims=True))
        mixed = jnp.dot(weights.astype(jnp.bfloat16), value_one, preferred_element_type=jnp.float32)
        return (mixed / norm_sum).astype(jnp.bfloat16)
    per_head = lax.map(one_head, jnp.arange(HQ, dtype=jnp.int32))
    return jnp.transpose(per_head, (1, 0, 2)).reshape(length, HQ * HD)
```

```python
import functools
import math

import jax
import jax.numpy as jnp
from jax import lax
from jax.experimental import pallas as pl
from jax.experimental.pallas import tpu as pltpu
from jax.sharding import Mesh, PartitionSpec as P

HQ = 128
KV = 8
HD = 128
TOKENS = 8192

ROWS = 32
MEMBERS = 16
HEADS = HQ // MEMBERS
BLOCK = 512
BIG = 2048
SMALL = 512
NEG_BIG = -1e30
SCALE = math.log2(math.e) / math.sqrt(HD)
SUM_LOW = 2.0**-90
SUM_HIGH = 2.0**120

NT = (((1,), (1,)), ((), ()))
NN = (((1,), (0,)), ((), ()))


def dot(a, b, dims):
    return lax.dot_general(a, b, dims, preferred_element_type=jnp.float32)


def token_start(x, y_hi, z, y_lo, core):
    return (y_lo * 2 + core) * 2048 + x * 512 + y_hi * 256 + z * 32


def attend_kernel(place, lag, q_ref, *refs):
    pieces, (out_ref, keys, values_t, query, acc, norm) = refs[:16], refs[16:]
    x, z, core = place[0], place[1], place[2]
    window_lag = lag[0]

    for offset in range(8):
        piece_z = (z + offset) % 8
        for swap in range(2):
            piece = pieces[offset * 2 + swap]
            for other in range(2):
                for member in range(8):
                    column = (x ^ other) ^ 0
                    low = jnp.minimum(column, 3 - column)
                    piece_x = low if member < 4 else 3 - low
                    start = token_start(
                        piece_x, (member // 2) % 2, piece_z, member % 2, core ^ swap
                    )
                    rows = pl.ds(pl.multiple_of(start, ROWS), ROWS)
                    key_rows = piece[other, member, :, :HD]
                    keys[rows, :HD] = key_rows
                    keys[rows, HD : 2 * HD] = key_rows
                    keys[rows, 2 * HD :] = piece[other, member, :, HD:]

    def turn(index, carry):
        start = pl.multiple_of(index * 512, 512)
        values_t[:, pl.ds(start, 512)] = keys[pl.ds(start, 512), 2 * HD :].T
        return carry

    lax.fori_loop(0, TOKENS // 512, turn, 0)

    def one_block(block, carry):
        xm, y_lo, source_core = block // 4, (block // 2) % 2, block % 2
        low = jnp.minimum(x, 3 - x)
        source_x = jnp.where(xm == 0, low, 3 - low)
        first = token_start(source_x, 0, z, y_lo, source_core)
        sources = [xm * 8 + y_hi * 4 + y_lo * 2 + source_core for y_hi in range(2)]
        for y_hi in range(2):
            for head in range(HEADS):
                rows = (y_hi * HEADS + head) * ROWS
                piece = q_ref[sources[y_hi], :, head * HD : (head + 1) * HD]
                scaled = piece.astype(jnp.float32) * SCALE
                high = scaled.astype(jnp.bfloat16)
                query[rows : rows + ROWS, :HD] = high
                query[rows : rows + ROWS, HD:] = (
                    scaled - high.astype(jnp.float32)
                ).astype(jnp.bfloat16)

        row = lax.broadcasted_iota(jnp.int32, (1, BLOCK), 1)
        last_key = first + window_lag + (row // (BLOCK // 2)) * 256 + row % ROWS
        all_see = jnp.minimum(first + window_lag + 1, TOKENS)
        some_see = jnp.minimum(first + 256 + ROWS + window_lag, TOKENS)
        big_steps = all_see // BIG
        small_first = big_steps * (BIG // SMALL)
        small_last = all_see // SMALL
        masked_last = (some_see + SMALL - 1) // SMALL

        acc[...] = jnp.zeros_like(acc)
        norm[...] = jnp.zeros_like(norm)

        def scores_of(start, size):
            return dot(keys[pl.ds(start, size), : 2 * HD], query[...], NT)

        def step(size, masked, index, carry):
            start = pl.multiple_of(index * size, size)
            scores = scores_of(start, size)
            if masked:
                key = start + lax.broadcasted_iota(jnp.int32, (size, 1), 0)
                scores = jnp.where(key <= last_key, scores, NEG_BIG)
            weights = jnp.exp2(scores)
            norm[...] += jnp.sum(weights.reshape(size // 8, 8, BLOCK), axis=0)
            acc[...] += dot(values_t[:, pl.ds(start, size)], weights.astype(jnp.bfloat16), NN)
            return carry

        lax.fori_loop(0, big_steps, functools.partial(step, BIG, False), 0)
        lax.fori_loop(small_first, small_last, functools.partial(step, SMALL, False), 0)
        lax.fori_loop(small_last, masked_last, functools.partial(step, SMALL, True), 0)

        total = jnp.sum(norm[...], axis=0, keepdims=True)
        in_range = jnp.where((total >= SUM_LOW) & (total <= SUM_HIGH), 1.0, 0.0)

        @pl.when(jnp.min(in_range) < 0.5)
        def _():
            acc[...] = jnp.zeros_like(acc)

            def careful(index, carry):
                peak, total = carry
                start = pl.multiple_of(index * SMALL, SMALL)
                scores = scores_of(start, SMALL)
                key = start + lax.broadcasted_iota(jnp.int32, (SMALL, 1), 0)
                scores = jnp.where(key <= last_key, scores, NEG_BIG)
                new_peak = jnp.maximum(peak, jnp.max(scores, axis=0, keepdims=True))
                factor = jnp.exp2(peak - new_peak)
                weights = jnp.exp2(scores - new_peak)
                acc[...] = acc[...] * factor + dot(
                    values_t[:, pl.ds(start, SMALL)], weights.astype(jnp.bfloat16), NN
                )
                return new_peak, total * factor + jnp.sum(weights, axis=0, keepdims=True)

            start = (jnp.full((1, BLOCK), NEG_BIG), jnp.zeros((1, BLOCK)))
            _, total = lax.fori_loop(0, masked_last, careful, start)
            norm[...] = jnp.zeros_like(norm)
            norm[:1] = total

        total = jnp.sum(norm[...], axis=0, keepdims=True)
        attended = (acc[...] / total).T.astype(jnp.bfloat16)
        for y_hi in range(2):
            for head in range(HEADS):
                rows = (y_hi * HEADS + head) * ROWS
                out_ref[sources[y_hi], :, head * HD : (head + 1) * HD] = attended[
                    rows : rows + ROWS
                ]
        return carry

    lax.fori_loop(0, MEMBERS // 2, one_block, 0)


def attend(place, lag, queries, pieces):
    smem = pl.BlockSpec(memory_space=pltpu.SMEM)
    vmem = pl.BlockSpec(memory_space=pltpu.VMEM)
    return pl.pallas_call(
        attend_kernel,
        out_shape=jax.ShapeDtypeStruct((MEMBERS, ROWS, HEADS * HD), jnp.bfloat16),
        in_specs=[smem, smem] + [vmem] * 17,
        out_specs=vmem,
        scratch_shapes=[
            pltpu.VMEM((TOKENS, 3 * HD), jnp.bfloat16),
            pltpu.VMEM((HD, TOKENS), jnp.bfloat16),
            pltpu.VMEM((BLOCK, 2 * HD), jnp.bfloat16),
            pltpu.VMEM((HD, BLOCK), jnp.float32),
            pltpu.VMEM((8, BLOCK), jnp.float32),
        ],
        compiler_params=pltpu.CompilerParams(vmem_limit_bytes=48 * 2**20),
        cost_estimate=pl.CostEstimate(
            flops=4 * HEADS * 512 * TOKENS * HD,
            bytes_accessed=6 * 2**20,
            transcendentals=HEADS * 512 * TOKENS,
        ),
    )(place, lag, queries, *pieces)


X_GROUPS = ((0, 3), (1, 2))


def member_groups(inner):
    return [[x * inner + i for x in pair for i in range(inner)] for pair in X_GROUPS]


def body(queries, keys, values, window_lag):
    x, z, core = (lax.axis_index(name) for name in ("x", "z", "core"))
    own_kv = jnp.concatenate(
        [keys.reshape(ROWS, KV, HD), values.reshape(ROWS, KV, HD)], axis=2
    ).transpose(1, 0, 2)
    own_kv = lax.all_to_all(
        own_kv,
        ("x", "y_hi", "y_lo"),
        split_axis=0,
        concat_axis=0,
        tiled=True,
        axis_index_groups=member_groups(4),
    )
    beside = lax.ppermute(own_kv, "x", [(i, i ^ 1) for i in range(4)])
    held = jnp.stack([own_kv, beside])
    up = [(i, (i + 1) % 8) for i in range(8)]
    down = [(i, (i - 1) % 8) for i in range(8)]
    by_offset = {0: held}
    from_below, from_above = held, held
    for step in range(1, 4):
        from_below = lax.ppermute(from_below, "z", up)
        from_above = lax.ppermute(from_above, "z", down)
        by_offset[8 - step] = from_below
        by_offset[step] = from_above
    by_offset[4] = jnp.stack(
        [lax.ppermute(from_below[0], "z", up), lax.ppermute(from_above[1], "z", down)]
    )
    pieces = []
    for offset in range(8):
        pieces.append(by_offset[offset])
        pieces.append(lax.ppermute(by_offset[offset], "core", [(0, 1), (1, 0)]))

    regroup = functools.partial(
        lax.all_to_all,
        axis_name=("x", "y_hi", "y_lo", "core"),
        split_axis=0,
        concat_axis=0,
        tiled=True,
        axis_index_groups=member_groups(8),
    )
    moved = regroup(queries.reshape(ROWS, MEMBERS, HEADS * HD).transpose(1, 0, 2))
    place = jnp.stack([x, z, core]).astype(jnp.int32)
    attended = attend(place, window_lag, moved, pieces)
    returned = regroup(attended)
    return returned.transpose(1, 0, 2).reshape(ROWS, HQ * HD)


def solution(mesh):
    fine = Mesh(mesh.devices.reshape(4, 2, 8, 2, 2), ("x", "y_hi", "z", "y_lo", "core"))
    spec = P(("y_lo", "core", "x", "y_hi", "z"), None)
    return jax.shard_map(
        body, mesh=fine, in_specs=(spec, spec, spec, P()), out_specs=spec, check_vma=False
    )
```

```python
import functools
import math

import jax
import jax.numpy as jnp
from jax import lax
from jax.experimental import pallas as pl
from jax.experimental.pallas import tpu as pltpu
from jax.sharding import Mesh, PartitionSpec as P

HQ = 128
KV = 8
HD = 128
TOKENS = 8192

ROWS = 32
MEMBERS = 16
HEADS = HQ // MEMBERS
BLOCK = 512
BIG = 2048
SMALL = 512
NEG_BIG = -1e30
SCALE = math.log2(math.e) / math.sqrt(HD)
SUM_LOW = 2.0**-90
SUM_HIGH = 2.0**120

NT = (((1,), (1,)), ((), ()))
NN = (((1,), (0,)), ((), ()))


def dot(a, b, dims):
    return lax.dot_general(a, b, dims, preferred_element_type=jnp.float32)


def token_start(x, y_hi, z, y_lo, core):
    return (y_lo * 2 + core) * 2048 + x * 512 + y_hi * 256 + z * 32


def attend_kernel(place, lag, q_ref, *refs):
    pieces, (out_ref, keys, values_t, query, acc, norm) = refs[:16], refs[16:]
    x, z, core = place[0], place[1], place[2]
    window_lag = lag[0]

    for offset in range(8):
        piece_z = (z + offset) % 8
        for swap in range(2):
            piece = pieces[offset * 2 + swap]
            for source in range(16):
                start = token_start(
                    source // 4, source // 2 % 2, piece_z, source % 2, core ^ swap
                )
                rows = pl.ds(pl.multiple_of(start, ROWS), ROWS)
                key_rows = piece[source, :, :HD]
                keys[rows, :HD] = key_rows
                keys[rows, HD : 2 * HD] = key_rows
                keys[rows, 2 * HD :] = piece[source, :, HD:]

    def turn(index, carry):
        start = pl.multiple_of(index * 512, 512)
        values_t[:, pl.ds(start, 512)] = keys[pl.ds(start, 512), 2 * HD :].T
        return carry

    lax.fori_loop(0, TOKENS // 512, turn, 0)

    def one_block(block, carry):
        xm, y_lo, source_core = block // 4, (block // 2) % 2, block % 2
        low = jnp.minimum(x, 3 - x)
        source_x = jnp.where(xm == 0, low, 3 - low)
        first = token_start(source_x, 0, z, y_lo, source_core)
        sources = [xm * 8 + y_hi * 4 + y_lo * 2 + source_core for y_hi in range(2)]
        for y_hi in range(2):
            for head in range(HEADS):
                rows = (y_hi * HEADS + head) * ROWS
                piece = q_ref[sources[y_hi], :, head * HD : (head + 1) * HD]
                scaled = piece.astype(jnp.float32) * SCALE
                high = scaled.astype(jnp.bfloat16)
                query[rows : rows + ROWS, :HD] = high
                query[rows : rows + ROWS, HD:] = (
                    scaled - high.astype(jnp.float32)
                ).astype(jnp.bfloat16)

        row = lax.broadcasted_iota(jnp.int32, (1, BLOCK), 1)
        last_key = first + window_lag + (row // (BLOCK // 2)) * 256 + row % ROWS
        all_see = jnp.minimum(first + window_lag + 1, TOKENS)
        some_see = jnp.minimum(first + 256 + ROWS + window_lag, TOKENS)
        big_steps = all_see // BIG
        small_first = big_steps * (BIG // SMALL)
        small_last = all_see // SMALL
        masked_last = (some_see + SMALL - 1) // SMALL

        acc[...] = jnp.zeros_like(acc)
        norm[...] = jnp.zeros_like(norm)

        def scores_of(start, size):
            return dot(keys[pl.ds(start, size), : 2 * HD], query[...], NT)

        def step(size, masked, index, carry):
            start = pl.multiple_of(index * size, size)
            scores = scores_of(start, size)
            if masked:
                key = start + lax.broadcasted_iota(jnp.int32, (size, 1), 0)
                scores = jnp.where(key <= last_key, scores, NEG_BIG)
            weights = jnp.exp2(scores)
            norm[...] += jnp.sum(weights.reshape(size // 8, 8, BLOCK), axis=0)
            acc[...] += dot(values_t[:, pl.ds(start, size)], weights.astype(jnp.bfloat16), NN)
            return carry

        lax.fori_loop(0, big_steps, functools.partial(step, BIG, False), 0)
        lax.fori_loop(small_first, small_last, functools.partial(step, SMALL, False), 0)
        lax.fori_loop(small_last, masked_last, functools.partial(step, SMALL, True), 0)

        total = jnp.sum(norm[...], axis=0, keepdims=True)
        in_range = jnp.where((total >= SUM_LOW) & (total <= SUM_HIGH), 1.0, 0.0)

        @pl.when(jnp.min(in_range) < 0.5)
        def _():
            acc[...] = jnp.zeros_like(acc)

            def careful(index, carry):
                peak, total = carry
                start = pl.multiple_of(index * SMALL, SMALL)
                scores = scores_of(start, SMALL)
                key = start + lax.broadcasted_iota(jnp.int32, (SMALL, 1), 0)
                scores = jnp.where(key <= last_key, scores, NEG_BIG)
                new_peak = jnp.maximum(peak, jnp.max(scores, axis=0, keepdims=True))
                factor = jnp.exp2(peak - new_peak)
                weights = jnp.exp2(scores - new_peak)
                acc[...] = acc[...] * factor + dot(
                    values_t[:, pl.ds(start, SMALL)], weights.astype(jnp.bfloat16), NN
                )
                return new_peak, total * factor + jnp.sum(weights, axis=0, keepdims=True)

            start = (jnp.full((1, BLOCK), NEG_BIG), jnp.zeros((1, BLOCK)))
            _, total = lax.fori_loop(0, masked_last, careful, start)
            norm[...] = jnp.zeros_like(norm)
            norm[:1] = total

        total = jnp.sum(norm[...], axis=0, keepdims=True)
        attended = (acc[...] / total).T.astype(jnp.bfloat16)
        for y_hi in range(2):
            for head in range(HEADS):
                rows = (y_hi * HEADS + head) * ROWS
                out_ref[sources[y_hi], :, head * HD : (head + 1) * HD] = attended[
                    rows : rows + ROWS
                ]
        return carry

    lax.fori_loop(0, MEMBERS // 2, one_block, 0)


def attend(place, lag, queries, pieces):
    smem = pl.BlockSpec(memory_space=pltpu.SMEM)
    vmem = pl.BlockSpec(memory_space=pltpu.VMEM)
    return pl.pallas_call(
        attend_kernel,
        out_shape=jax.ShapeDtypeStruct((MEMBERS, ROWS, HEADS * HD), jnp.bfloat16),
        in_specs=[smem, smem] + [vmem] * 17,
        out_specs=vmem,
        scratch_shapes=[
            pltpu.VMEM((TOKENS, 3 * HD), jnp.bfloat16),
            pltpu.VMEM((HD, TOKENS), jnp.bfloat16),
            pltpu.VMEM((BLOCK, 2 * HD), jnp.bfloat16),
            pltpu.VMEM((HD, BLOCK), jnp.float32),
            pltpu.VMEM((8, BLOCK), jnp.float32),
        ],
        compiler_params=pltpu.CompilerParams(vmem_limit_bytes=48 * 2**20),
        cost_estimate=pl.CostEstimate(
            flops=4 * HEADS * 512 * TOKENS * HD,
            bytes_accessed=6 * 2**20,
            transcendentals=HEADS * 512 * TOKENS,
        ),
    )(place, lag, queries, *pieces)


X_GROUPS = ((0, 3), (1, 2))


def member_groups(inner):
    return [[x * inner + i for x in pair for i in range(inner)] for pair in X_GROUPS]


def body(queries, keys, values, window_lag):
    x, z, core = (lax.axis_index(name) for name in ("x", "z", "core"))
    kv = jnp.concatenate(
        [keys.reshape(ROWS, KV, HD), values.reshape(ROWS, KV, HD)], axis=2
    ).transpose(1, 0, 2)
    by_chip = jnp.broadcast_to(kv.reshape(2, 1, 4, ROWS, 2 * HD), (2, 2, 4, ROWS, 2 * HD))
    held = lax.all_to_all(
        by_chip.reshape(16, ROWS, 2 * HD),
        ("x", "y_hi", "y_lo"),
        split_axis=0,
        concat_axis=0,
        tiled=True,
    )
    regroup = functools.partial(
        lax.all_to_all,
        axis_name=("x", "y_hi", "y_lo", "core"),
        split_axis=0,
        concat_axis=0,
        tiled=True,
        axis_index_groups=member_groups(8),
    )
    by_member = queries.reshape(ROWS, MEMBERS, HEADS * HD).transpose(1, 0, 2)
    by_member, held = lax.optimization_barrier((by_member, held))
    moved = regroup(by_member)
    up = [(i, (i + 1) % 8) for i in range(8)]
    down = [(i, (i - 1) % 8) for i in range(8)]
    by_offset = {0: held}
    from_below, from_above = held, held
    for step in range(1, 4):
        if step == 4:
            from_below, from_above, moved = lax.optimization_barrier(
                (from_below, from_above, moved)
            )
        from_below = lax.ppermute(from_below, "z", up)
        from_above = lax.ppermute(from_above, "z", down)
        by_offset[8 - step] = from_below
        by_offset[step] = from_above
    from_below, from_above, moved = lax.optimization_barrier((from_below, from_above, moved))
    by_offset[4] = jnp.concatenate(
        [lax.ppermute(from_below[:8], "z", up), lax.ppermute(from_above[8:], "z", down)]
    )
    pieces = []
    for offset in range(8):
        pieces.append(by_offset[offset])
        pieces.append(lax.ppermute(by_offset[offset], "core", [(0, 1), (1, 0)]))

    place = jnp.stack([x, z, core]).astype(jnp.int32)
    attended = attend(place, window_lag, moved, pieces)
    returned = regroup(attended)
    return returned.transpose(1, 0, 2).reshape(ROWS, HQ * HD)


def solution(mesh):
    fine = Mesh(mesh.devices.reshape(4, 2, 8, 2, 2), ("x", "y_hi", "z", "y_lo", "core"))
    spec = P(("y_lo", "core", "x", "y_hi", "z"), None)
    return jax.shard_map(
        body, mesh=fine, in_specs=(spec, spec, spec, P()), out_specs=spec, check_vma=False
    )
```

```python
import functools
import math

import jax
import jax.numpy as jnp
from jax import lax
from jax.experimental import pallas as pl
from jax.experimental.pallas import tpu as pltpu
from jax.sharding import Mesh, PartitionSpec as P

HQ = 128
KV = 8
HD = 128
TOKENS = 8192

ROWS = 32
MEMBERS = 16
HEADS = HQ // MEMBERS
BLOCK = 512
BLOCKS = 8
UNIT = 1024
RUN = 128
UNITS = TOKENS // UNIT
SLOTS = (3, 2, 3)
NEG_BIG = -1e30
SCALE = math.log2(math.e) / math.sqrt(HD)
SUM_LOW = 2.0**-90
SUM_HIGH = 2.0**120

NT = (((1,), (1,)), ((), ()))
NN = (((1,), (0,)), ((), ()))


def dot(a, b, dims):
    return lax.dot_general(a, b, dims, preferred_element_type=jnp.float32)


def origins(place):
    z, core = place[1], place[2]
    toward = core * 2 - 1
    found = [(z, core)]
    for distance in range(1, 4):
        for ring in range(2):
            found.append(((z + 8 + (1 - 2 * ring) * toward * distance) % 8, core ^ ring))
    return found + [((z + 4) % 8, core)]


def attend_kernel(phase, *refs):
    first, last = phase == 0, phase == 2
    slots = SLOTS[phase]
    held = slots * RUN
    count = (3, 2, 4)[phase]
    place, pieces, refs = refs[0], refs[1 : 1 + count], refs[1 + count :]
    if first:
        q_ref, acc, norm, query, keys, values_t, places = refs
    elif not last:
        query, _, _, acc, norm, keys, values_t, places = refs
    else:
        (query, acc, norm), earlier, refs = refs[:3], refs[3:8], refs[8:]
        out_ref, keys, values_t, places, spare, spare_acc = refs
    x, z, core, window_lag = place[0], place[1], place[2], place[3]
    base = sum(SLOTS[:phase])

    row = lax.broadcasted_iota(jnp.int32, (RUN, HD), 0)
    row = row // ROWS * 256 + row % ROWS
    for slot in range(slots):
        piece_z, piece_core = origins(place)[base + slot]
        tokens = row + piece_z * ROWS
        places[slot * RUN : (slot + 1) * RUN, :] = tokens
        places[held + slot * RUN : held + (slot + 1) * RUN, :] = tokens + UNIT
        for swap in range(2):
            piece = pieces[slot + swap] if last and slot == 2 else pieces[slot].at[swap]
            for part in range(4):
                unit = part // 2 * 4 + (piece_core ^ swap) * 2 + part % 2
                rows = pl.ds(pl.multiple_of(unit * held + slot * RUN, RUN), RUN)
                run = piece[part * 4 : part * 4 + 4].reshape(RUN, 2 * HD)
                keys[rows, :HD] = run[:, :HD]
                keys[rows, HD:] = run[:, :HD]
                values_t[:, rows] = run[:, HD:].T

    def one_block(block, carry):
        xm, source_tp = block // 4, block % 4
        low = jnp.minimum(x, 3 - x)
        source_x = jnp.where(xm == 0, low, 3 - low)
        first_token = source_tp * 2048 + source_x * 512 + z * ROWS
        sources = [xm * 8 + y_hi * 4 + source_tp for y_hi in range(2)]
        if first:
            for y_hi in range(2):
                for head in range(HEADS):
                    rows = (y_hi * HEADS + head) * ROWS
                    part = q_ref[sources[y_hi], :, head * HD : (head + 1) * HD]
                    scaled = part.astype(jnp.float32) * SCALE
                    high = scaled.astype(jnp.bfloat16)
                    rest = scaled - high.astype(jnp.float32)
                    query[block, rows : rows + ROWS, :HD] = high
                    query[block, rows : rows + ROWS, HD:] = rest.astype(jnp.bfloat16)
            acc[block] = jnp.zeros((HD, BLOCK), jnp.float32)
            norm[block] = jnp.zeros((8, BLOCK), jnp.float32)

        row = lax.broadcasted_iota(jnp.int32, (1, BLOCK), 1)
        last_key = first_token + window_lag + (row // (BLOCK // 2)) * 256 + row % ROWS
        all_see = jnp.minimum(first_token + window_lag + 1, TOKENS)
        some_see = jnp.minimum(first_token + 256 + ROWS + window_lag, TOKENS)
        whole = all_see // UNIT
        some = (some_see + UNIT - 1) // UNIT

        def scores_of(start, size):
            return dot(keys[pl.ds(start, size), :], query[block], NT)

        def add(scores, turned):
            weights = jnp.exp2(scores)
            size = scores.shape[0]
            norm[block] += jnp.sum(weights.reshape(size // 8, 8, BLOCK), axis=0)
            acc[block] += dot(turned, weights.astype(jnp.bfloat16), NN)

        def step(unit, units, masked=False):
            start = pl.multiple_of(unit * held, 2 * held)
            size = units * held
            scores = scores_of(start, size)
            if masked:
                seen = jnp.concatenate([places[...]] * (BLOCK // HD), axis=1)
                scores = jnp.where(seen <= last_key - unit * UNIT, scores, NEG_BIG)
            add(scores, values_t[:, pl.ds(start, size)])

        @pl.when(whole == UNITS)
        def _():
            step(0, UNITS)

        @pl.when((whole >= 4) & (whole < UNITS))
        def _():
            step(0, 4)

        def edge(pair, carry):
            step(pair * 2, 2, True)
            return carry

        lax.fori_loop(whole // 4 * 2, (some + 1) // 2, edge, 0)
        if not last:
            return carry

        total = jnp.sum(norm[block], axis=0, keepdims=True)
        in_range = jnp.where((total >= SUM_LOW) & (total <= SUM_HIGH), 1.0, 0.0)
        fine = jnp.min(in_range) > 0.5

        def give(mixed, total):
            attended = (mixed / total).T.astype(jnp.bfloat16)
            for y_hi in range(2):
                for head in range(HEADS):
                    rows = (y_hi * HEADS + head) * ROWS
                    out_ref[sources[y_hi], :, head * HD : (head + 1) * HD] = attended[
                        rows : rows + ROWS
                    ]

        @pl.when(fine)
        def _():
            give(acc[block], total)

        @pl.when(jnp.logical_not(fine))
        def _():
            for index, piece in enumerate(earlier + pieces[:2]):
                pltpu.sync_copy(piece, spare.at[index])
            for swap in range(2):
                pltpu.sync_copy(pieces[2 + swap], spare.at[7, swap])
            spare_acc[...] = jnp.zeros_like(spare_acc)

            def careful(index, carry):
                peak, total = carry
                piece_z, piece_core = jnp.int32(0), jnp.int32(0)
                for slot, (slot_z, slot_core) in enumerate(origins(place)):
                    piece_z = jnp.where(index // 2 == slot, slot_z, piece_z)
                    piece_core = jnp.where(index // 2 == slot, slot_core, piece_core)
                run = spare[index // 2, index % 2].reshape(4 * RUN, 2 * HD)
                pair = jnp.concatenate([run[:, :HD]] * 2, axis=1)
                scores = dot(pair, query[block], NT)
                token = lax.broadcasted_iota(jnp.int32, (4 * RUN, HD), 0)
                token = token // (2 * RUN) * 4096 + token // ROWS % 8 * 256 + token % ROWS
                token = token + (piece_core ^ (index % 2)) * 2048 + piece_z * ROWS
                seen = jnp.concatenate([token] * (BLOCK // HD), axis=1) <= last_key
                scores = jnp.where(seen, scores, NEG_BIG)
                new_peak = jnp.maximum(peak, jnp.max(scores, axis=0, keepdims=True))
                factor = jnp.exp2(peak - new_peak)
                weights = jnp.where(seen, jnp.exp2(scores - new_peak), 0.0)
                mixed = dot(run[:, HD:].T, weights.astype(jnp.bfloat16), NN)
                spare_acc[...] = spare_acc[...] * factor + mixed
                return new_peak, total * factor + jnp.sum(weights, axis=0, keepdims=True)

            start = (jnp.full((1, BLOCK), NEG_BIG), jnp.zeros((1, BLOCK)))
            _, total = lax.fori_loop(0, 16, careful, start)
            give(spare_acc[...], total)

        return carry

    lax.fori_loop(0, BLOCKS, one_block, 0)


ACC = jax.ShapeDtypeStruct((BLOCKS, HD, BLOCK), jnp.float32)
NORM = jax.ShapeDtypeStruct((BLOCKS, 8, BLOCK), jnp.float32)
QUERY = jax.ShapeDtypeStruct((BLOCKS, BLOCK, 2 * HD), jnp.bfloat16)
OUT = jax.ShapeDtypeStruct((MEMBERS, ROWS, HEADS * HD), jnp.bfloat16)


def attend(phase, place, pieces, state, earlier=()):
    smem = pl.BlockSpec(memory_space=pltpu.SMEM)
    vmem = pl.BlockSpec(memory_space=pltpu.VMEM)
    in_specs = [smem] + [vmem] * (len(pieces) + len(state))
    in_specs += [pl.BlockSpec(memory_space=pl.ANY)] * len(earlier)
    total_keys = UNITS * SLOTS[phase] * RUN
    scratch = [
        pltpu.VMEM((total_keys, 2 * HD), jnp.bfloat16),
        pltpu.VMEM((HD, total_keys), jnp.bfloat16),
        pltpu.VMEM((2 * SLOTS[phase] * RUN, HD), jnp.int32),
    ]
    if phase == 2:
        scratch += [
            pltpu.VMEM((8, 2, 16, ROWS, 2 * HD), jnp.bfloat16),
            pltpu.VMEM((HD, BLOCK), jnp.float32),
        ]
    out_shape = ((ACC, NORM, QUERY), (ACC, NORM), OUT)[phase]
    aliases = {len(pieces) + 2: 0, len(pieces) + 3: 1} if phase == 1 else {}
    return pl.pallas_call(
        functools.partial(attend_kernel, phase),
        out_shape=out_shape,
        in_specs=in_specs,
        out_specs=jax.tree.map(lambda _: vmem, out_shape),
        scratch_shapes=scratch,
        input_output_aliases=aliases,
        compiler_params=pltpu.CompilerParams(vmem_limit_bytes=32 * 2**20),
        cost_estimate=pl.CostEstimate(
            flops=8 * BLOCKS * BLOCK * total_keys * HD,
            bytes_accessed=2**20,
            transcendentals=BLOCKS * BLOCK * total_keys,
        ),
    )(place, *pieces, *state, *earlier)


def pack_kernel(keys_ref, values_ref, out_ref):
    for chip in range(16):
        group = chip // 4 % 2 * 4 + chip % 2 * 2 + chip // 8
        columns = slice(group * HD, (group + 1) * HD)
        out_ref[chip, :, :HD] = keys_ref[:, columns]
        out_ref[chip, :, HD:] = values_ref[:, columns]


X_GROUPS = ((0, 3), (1, 2))
PAIR_MEMBERS = [[x * 8 + i for x in pair for i in range(8)] for pair in X_GROUPS]


def body(queries, keys, values, window_lag):
    x, z, core = (lax.axis_index(name) for name in ("x", "z", "core"))
    kv = pl.pallas_call(
        pack_kernel,
        out_shape=jax.ShapeDtypeStruct((16, ROWS, 2 * HD), jnp.bfloat16),
    )(keys, values)
    held = lax.all_to_all(
        kv, ("y_lo", "x", "y_hi"), split_axis=0, concat_axis=0, tiled=True
    )
    regroup = functools.partial(
        lax.all_to_all,
        axis_name=("x", "y_hi", "y_lo", "core"),
        split_axis=0,
        concat_axis=0,
        tiled=True,
        axis_index_groups=PAIR_MEMBERS,
    )
    by_member = queries.reshape(ROWS, MEMBERS, HEADS * HD).transpose(1, 0, 2)
    by_member, held = lax.optimization_barrier((by_member, held))
    moved = regroup(by_member)

    def other_core(piece):
        return lax.ppermute(piece, "core", [(0, 1), (1, 0)])

    def onward(piece):
        up = [(i * 2, (i + 1) % 8 * 2) for i in range(8)]
        down = [(i * 2 + 1, (i - 1) % 8 * 2 + 1) for i in range(8)]
        return lax.ppermute(piece, ("z", "core"), up + down)

    def both(piece):
        return [piece, other_core(piece)]

    place = jnp.concatenate([jnp.stack([x, z, core]).astype(jnp.int32), window_lag])
    chip = jnp.stack(both(held))
    came1 = onward(chip)
    came2 = onward(came1)
    came2, moved = lax.optimization_barrier((came2, moved))
    came3 = onward(came2)
    near, middle = [chip, *both(came1)], both(came2)
    acc, norm, query = attend(0, place, near, (moved,))
    came3, acc = lax.optimization_barrier((came3, acc))
    opposite = onward(came3[0])
    far = both(came3)
    acc, norm = attend(1, place, middle, (query, acc, norm))
    opposite, acc = lax.optimization_barrier((opposite, acc))
    far += both(opposite)
    attended = attend(2, place, far, (query, acc, norm), near + middle)
    returned = regroup(attended)
    return returned.transpose(1, 0, 2).reshape(ROWS, HQ * HD)


def solution(mesh):
    fine = Mesh(mesh.devices.reshape(4, 2, 8, 2, 2), ("x", "y_hi", "z", "y_lo", "core"))
    spec = P(("y_lo", "core", "x", "y_hi", "z"), None)
    return jax.shard_map(
        body, mesh=fine, in_specs=(spec, spec, spec, P()), out_specs=spec, check_vma=False
    )
```

```python
import functools
import math

import jax
import jax.numpy as jnp
from jax import lax
from jax.experimental import pallas as pl
from jax.experimental.pallas import tpu as pltpu
from jax.sharding import Mesh, PartitionSpec as P

HQ = 128
KV = 8
HD = 128
TOKENS = 8192

ROWS = 32
MEMBERS = 16
HEADS = HQ // MEMBERS
BLOCK = 1024
BLOCKS = 4
UNIT = 1024
RUN = 128
UNITS = TOKENS // UNIT
SLOTS = (3, 2, 3)
NEG_BIG = -1e30
SCALE = math.log2(math.e) / math.sqrt(HD)
SUM_LOW = 2.0**-90
SUM_HIGH = 2.0**120

NT = (((1,), (1,)), ((), ()))
NN = (((1,), (0,)), ((), ()))


def dot(a, b, dims):
    return lax.dot_general(a, b, dims, preferred_element_type=jnp.float32)


def origins(place):
    z, core = place[1], place[2]
    toward = core * 2 - 1
    found = [(z, core)]
    for distance in range(1, 4):
        for ring in range(2):
            found.append(((z + 8 + (1 - 2 * ring) * toward * distance) % 8, core ^ ring))
    return found + [((z + 4) % 8, core)]


def attend_kernel(phase, *refs):
    first, last = phase == 0, phase == 2
    slots = SLOTS[phase]
    held = slots * RUN
    count = (3, 2, 4)[phase]
    place, pieces, refs = refs[0], refs[1 : 1 + count], refs[1 + count :]
    if first:
        q_ref, acc, norm, keys, values_t, places, query = refs
    elif not last:
        q_ref, _, _, acc, norm, keys, values_t, places, query = refs
    else:
        (q_ref, acc, norm), earlier, refs = refs[:3], refs[3:8], refs[8:]
        out_ref, keys, values_t, places, query, spare, spare_acc = refs
    x, z, core, window_lag = place[0], place[1], place[2], place[3]
    base = sum(SLOTS[:phase])

    row = lax.broadcasted_iota(jnp.int32, (RUN, HD), 0)
    row = row // ROWS * 256 + row % ROWS
    for slot in range(slots):
        piece_z, piece_core = origins(place)[base + slot]
        tokens = row + piece_z * ROWS
        places[slot * RUN : (slot + 1) * RUN, :] = tokens
        places[held + slot * RUN : held + (slot + 1) * RUN, :] = tokens + UNIT
        for swap in range(2):
            piece = pieces[slot + swap] if last and slot == 2 else pieces[slot].at[swap]
            for part in range(4):
                unit = part // 2 * 4 + (piece_core ^ swap) * 2 + part % 2
                rows = pl.ds(pl.multiple_of(unit * held + slot * RUN, RUN), RUN)
                run = piece[part * 4 : part * 4 + 4].reshape(RUN, 2 * HD)
                keys[rows, :] = run[:, :HD]
                values_t[:, rows] = run[:, HD:].T

    def one_block(block, carry):
        low = jnp.minimum(x, 3 - x)
        first_token = block * 2048 + z * ROWS
        sources = [pair * 4 + block for pair in range(4)]
        pairs = [(pair, head) for pair in range(4) for head in range(HEADS)]
        for index, (pair, head) in enumerate(pairs):
            part = q_ref[sources[pair], :, head * HD : (head + 1) * HD]
            query[index * ROWS : (index + 1) * ROWS, :] = part
        if first:
            acc[block] = jnp.zeros((HD, BLOCK), jnp.float32)
            norm[block] = jnp.zeros((8, BLOCK), jnp.float32)

        row = lax.broadcasted_iota(jnp.int32, (1, BLOCK), 1)
        source_x = jnp.where(row < BLOCK // 2, low, 3 - low)
        last_key = first_token + window_lag + row % ROWS
        last_key = last_key + source_x * 512 + row // (BLOCK // 4) % 2 * 256
        all_see = jnp.minimum(first_token + low * 512 + window_lag + 1, TOKENS)
        some_see = first_token + (3 - low) * 512 + 256 + ROWS + window_lag
        some_see = jnp.minimum(some_see, TOKENS)
        whole = all_see // UNIT
        some = (some_see + UNIT - 1) // UNIT

        def scores_of(start, size):
            return dot(keys[pl.ds(start, size), :], query[...], NT) * SCALE

        def add(scores, turned):
            weights = jnp.exp2(scores)
            size = scores.shape[0]
            norm[block] += jnp.sum(weights.reshape(size // 8, 8, BLOCK), axis=0)
            acc[block] += dot(turned, weights.astype(jnp.bfloat16), NN)

        def step(unit, units, masked=False):
            start = pl.multiple_of(unit * held, 2 * held)
            size = units * held
            scores = scores_of(start, size)
            if masked:
                seen = jnp.concatenate([places[...]] * (BLOCK // HD), axis=1)
                scores = jnp.where(seen <= last_key - unit * UNIT, scores, NEG_BIG)
            add(scores, values_t[:, pl.ds(start, size)])

        @pl.when(whole == UNITS)
        def _():
            step(0, UNITS)

        @pl.when((whole >= 4) & (whole < UNITS))
        def _():
            step(0, 4)

        def edge(pair, carry):
            step(pair * 2, 2, True)
            return carry

        lax.fori_loop(whole // 4 * 2, (some + 1) // 2, edge, 0)
        if not last:
            return carry

        total = jnp.sum(norm[block], axis=0, keepdims=True)
        in_range = jnp.where((total >= SUM_LOW) & (total <= SUM_HIGH), 1.0, 0.0)
        fine = jnp.min(in_range) > 0.5

        def give(mixed, total):
            attended = (mixed / total).T.astype(jnp.bfloat16)
            for index, (pair, head) in enumerate(pairs):
                rows = attended[index * ROWS : (index + 1) * ROWS]
                out_ref[sources[pair], :, head * HD : (head + 1) * HD] = rows

        @pl.when(fine)
        def _():
            give(acc[block], total)

        @pl.when(jnp.logical_not(fine))
        def _():
            for index, piece in enumerate(earlier + pieces[:2]):
                pltpu.sync_copy(piece, spare.at[index])
            for swap in range(2):
                pltpu.sync_copy(pieces[2 + swap], spare.at[7, swap])
            spare_acc[...] = jnp.zeros_like(spare_acc)

            def careful(index, carry):
                peak, total = carry
                piece_z, piece_core = jnp.int32(0), jnp.int32(0)
                for slot, (slot_z, slot_core) in enumerate(origins(place)):
                    piece_z = jnp.where(index // 2 == slot, slot_z, piece_z)
                    piece_core = jnp.where(index // 2 == slot, slot_core, piece_core)
                run = spare[index // 2, index % 2].reshape(4 * RUN, 2 * HD)
                scores = dot(run[:, :HD], query[...], NT) * SCALE
                token = lax.broadcasted_iota(jnp.int32, (4 * RUN, HD), 0)
                token = token // (2 * RUN) * 4096 + token // ROWS % 8 * 256 + token % ROWS
                token = token + (piece_core ^ (index % 2)) * 2048 + piece_z * ROWS
                seen = jnp.concatenate([token] * (BLOCK // HD), axis=1) <= last_key
                scores = jnp.where(seen, scores, NEG_BIG)
                new_peak = jnp.maximum(peak, jnp.max(scores, axis=0, keepdims=True))
                factor = jnp.exp2(peak - new_peak)
                weights = jnp.where(seen, jnp.exp2(scores - new_peak), 0.0)
                mixed = dot(run[:, HD:].T, weights.astype(jnp.bfloat16), NN)
                spare_acc[...] = spare_acc[...] * factor + mixed
                return new_peak, total * factor + jnp.sum(weights, axis=0, keepdims=True)

            start = (jnp.full((1, BLOCK), NEG_BIG), jnp.zeros((1, BLOCK)))
            _, total = lax.fori_loop(0, 16, careful, start)
            give(spare_acc[...], total)

        return carry

    lax.fori_loop(0, BLOCKS, one_block, 0)


ACC = jax.ShapeDtypeStruct((BLOCKS, HD, BLOCK), jnp.float32)
NORM = jax.ShapeDtypeStruct((BLOCKS, 8, BLOCK), jnp.float32)
OUT = jax.ShapeDtypeStruct((MEMBERS, ROWS, HEADS * HD), jnp.bfloat16)


def attend(phase, place, pieces, state, earlier=()):
    smem = pl.BlockSpec(memory_space=pltpu.SMEM)
    vmem = pl.BlockSpec(memory_space=pltpu.VMEM)
    in_specs = [smem] + [vmem] * (len(pieces) + len(state))
    in_specs += [pl.BlockSpec(memory_space=pl.ANY)] * len(earlier)
    total_keys = UNITS * SLOTS[phase] * RUN
    scratch = [
        pltpu.VMEM((total_keys, HD), jnp.bfloat16),
        pltpu.VMEM((HD, total_keys), jnp.bfloat16),
        pltpu.VMEM((2 * SLOTS[phase] * RUN, HD), jnp.int32),
        pltpu.VMEM((BLOCK, HD), jnp.bfloat16),
    ]
    if phase == 2:
        scratch += [
            pltpu.VMEM((8, 2, 16, ROWS, 2 * HD), jnp.bfloat16),
            pltpu.VMEM((HD, BLOCK), jnp.float32),
        ]
    out_shape = ((ACC, NORM), (ACC, NORM), OUT)[phase]
    aliases = {len(pieces) + 2: 0, len(pieces) + 3: 1} if phase == 1 else {}
    return pl.pallas_call(
        functools.partial(attend_kernel, phase),
        out_shape=out_shape,
        in_specs=in_specs,
        out_specs=jax.tree.map(lambda _: vmem, out_shape),
        scratch_shapes=scratch,
        input_output_aliases=aliases,
        compiler_params=pltpu.CompilerParams(vmem_limit_bytes=44 * 2**20),
        cost_estimate=pl.CostEstimate(
            flops=8 * BLOCKS * BLOCK * total_keys * HD,
            bytes_accessed=2**20,
            transcendentals=BLOCKS * BLOCK * total_keys,
        ),
    )(place, *pieces, *state, *earlier)


def pack_kernel(keys_ref, values_ref, out_ref):
    for chip in range(16):
        group = chip // 4 % 2 * 4 + chip % 2 * 2 + chip // 8
        columns = slice(group * HD, (group + 1) * HD)
        out_ref[chip, :, :HD] = keys_ref[:, columns]
        out_ref[chip, :, HD:] = values_ref[:, columns]


X_GROUPS = ((0, 3), (1, 2))
PAIR_MEMBERS = [[x * 8 + i for x in pair for i in range(8)] for pair in X_GROUPS]


def body(queries, keys, values, window_lag):
    x, z, core = (lax.axis_index(name) for name in ("x", "z", "core"))
    kv = pl.pallas_call(
        pack_kernel,
        out_shape=jax.ShapeDtypeStruct((16, ROWS, 2 * HD), jnp.bfloat16),
    )(keys, values)
    held = lax.all_to_all(
        kv, ("y_lo", "x", "y_hi"), split_axis=0, concat_axis=0, tiled=True
    )
    regroup = functools.partial(
        lax.all_to_all,
        axis_name=("x", "y_hi", "y_lo", "core"),
        split_axis=0,
        concat_axis=0,
        tiled=True,
        axis_index_groups=PAIR_MEMBERS,
    )
    by_member = queries.reshape(ROWS, MEMBERS, HEADS * HD).transpose(1, 0, 2)
    by_member, held = lax.optimization_barrier((by_member, held))
    moved = regroup(by_member)

    def other_core(piece):
        return lax.ppermute(piece, "core", [(0, 1), (1, 0)])

    def onward(piece):
        up = [(i * 2, (i + 1) % 8 * 2) for i in range(8)]
        down = [(i * 2 + 1, (i - 1) % 8 * 2 + 1) for i in range(8)]
        return lax.ppermute(piece, ("z", "core"), up + down)

    def both(piece):
        return [piece, other_core(piece)]

    place = jnp.concatenate([jnp.stack([x, z, core]).astype(jnp.int32), window_lag])
    chip = jnp.stack(both(held))
    came1 = onward(chip)
    came2 = onward(came1)
    came2, moved = lax.optimization_barrier((came2, moved))
    came3 = onward(came2)
    near, middle = [chip, *both(came1)], both(came2)
    acc, norm = attend(0, place, near, (moved,))
    came3, acc = lax.optimization_barrier((came3, acc))
    opposite = onward(came3[0])
    far = both(came3)
    acc, norm = attend(1, place, middle, (moved, acc, norm))
    opposite, acc = lax.optimization_barrier((opposite, acc))
    far += both(opposite)
    attended = attend(2, place, far, (moved, acc, norm), near + middle)
    returned = regroup(attended)
    return returned.transpose(1, 0, 2).reshape(ROWS, HQ * HD)


def solution(mesh):
    fine = Mesh(mesh.devices.reshape(4, 2, 8, 2, 2), ("x", "y_hi", "z", "y_lo", "core"))
    spec = P(("y_lo", "core", "x", "y_hi", "z"), None)
    return jax.shard_map(
        body, mesh=fine, in_specs=(spec, spec, spec, P()), out_specs=spec, check_vma=False
    )
```

```python
import functools
import math

import jax
import jax.numpy as jnp
from jax import lax
from jax.experimental import pallas as pl
from jax.experimental.pallas import tpu as pltpu
from jax.sharding import Mesh, PartitionSpec as P

HQ = 128
KV = 8
HD = 128
TOKENS = 8192

ROWS = 32
MEMBERS = 16
HEADS = HQ // MEMBERS
BLOCK = 1024
BLOCKS = 4
SIDE = BLOCK // 2
UNIT = 1024
RUN = 128
UNITS = TOKENS // UNIT
SLOTS = (3, 2, 3)
NEG_BIG = -1e30
SCALE = math.log2(math.e) / math.sqrt(HD)
SUM_LOW = 2.0**-90
SUM_HIGH = 2.0**120

NT = (((1,), (1,)), ((), ()))
NN = (((1,), (0,)), ((), ()))


def dot(a, b, dims):
    return lax.dot_general(a, b, dims, preferred_element_type=jnp.float32)


def origins(place):
    z, core = place[1], place[2]
    toward = core * 2 - 1
    found = [(z, core)]
    for distance in range(1, 4):
        for ring in range(2):
            found.append(((z + 8 + (1 - 2 * ring) * toward * distance) % 8, core ^ ring))
    return found + [((z + 4) % 8, core)]


def attend_kernel(phase, *refs):
    first, last = phase == 0, phase == 2
    slots = SLOTS[phase]
    held = slots * RUN
    count = (3, 2, 4)[phase]
    place, pieces, refs = refs[0], refs[1 : 1 + count], refs[1 + count :]
    if first:
        q_ref, acc, norm, keys, values_t, places, query = refs
    elif not last:
        q_ref, _, _, acc, norm, keys, values_t, places, query = refs
    else:
        (q_ref, acc, norm), earlier, refs = refs[:3], refs[3:8], refs[8:]
        out_ref, keys, values_t, places, query, spare, spare_acc = refs
    x, z, core, window_lag = place[0], place[1], place[2], place[3]
    base = sum(SLOTS[:phase])

    row = lax.broadcasted_iota(jnp.int32, (RUN, HD), 0)
    row = row // ROWS * 256 + row % ROWS
    for slot in range(slots):
        piece_z, piece_core = origins(place)[base + slot]
        tokens = row + piece_z * ROWS
        places[slot * RUN : (slot + 1) * RUN, :] = tokens
        places[held + slot * RUN : held + (slot + 1) * RUN, :] = tokens + UNIT
        for swap in range(2):
            piece = pieces[slot + swap] if last and slot == 2 else pieces[slot].at[swap]
            for part in range(4):
                unit = part // 2 * 4 + (piece_core ^ swap) * 2 + part % 2
                rows = pl.ds(pl.multiple_of(unit * held + slot * RUN, RUN), RUN)
                run = piece[part * 4 : part * 4 + 4].reshape(RUN, 2 * HD)
                keys[rows, :] = run[:, :HD]
                values_t[:, rows] = run[:, HD:].T

    def one_block(block, carry):
        low = jnp.minimum(x, 3 - x)
        first_token = block * 2048 + z * ROWS
        sources = [pair * 4 + block for pair in range(4)]
        pairs = [(pair, head) for pair in range(4) for head in range(HEADS)]
        for index, (pair, head) in enumerate(pairs):
            part = q_ref[sources[pair], :, head * HD : (head + 1) * HD]
            query[index * ROWS : (index + 1) * ROWS, :] = part
        if first:
            for side in range(2):
                acc[block * 2 + side] = jnp.zeros((HD, SIDE), jnp.float32)
                norm[block * 2 + side] = jnp.zeros((8, SIDE), jnp.float32)

        row = lax.broadcasted_iota(jnp.int32, (1, SIDE), 1)
        last_row = row // (SIDE // 2) * 256 + row % ROWS + window_lag

        def add(start, size, side, sides, seen=None):
            start = pl.multiple_of(start, 2 * held)
            first_row = pl.multiple_of(side * SIDE, SIDE)
            rows = query[pl.ds(first_row, sides * SIDE), :]
            scores = dot(keys[pl.ds(start, size), :], rows, NT) * SCALE
            if seen is not None:
                scores = jnp.where(seen, scores, NEG_BIG)
            weights = jnp.exp2(scores)
            summed = jnp.sum(weights.reshape(size // 8, 8, sides * SIDE), axis=0)
            mixed = dot(values_t[:, pl.ds(start, size)], weights.astype(jnp.bfloat16), NN)
            for part in range(sides):
                columns = slice(part * SIDE, (part + 1) * SIDE)
                norm[block * 2 + side + part] += summed[:, columns]
                acc[block * 2 + side + part] += mixed[:, columns]

        def one_side(side, carry):
            token = first_token + jnp.where(side == 0, low, 3 - low) * 512
            all_see = jnp.minimum(token + window_lag + 1, TOKENS)
            some_see = jnp.minimum(token + 256 + ROWS + window_lag, TOKENS)
            whole = all_see // UNIT
            some = (some_see + UNIT - 1) // UNIT

            @pl.when(whole == UNITS)
            def _():
                add(0, UNITS * held, side, 1)

            @pl.when((whole >= 4) & (whole < UNITS))
            def _():
                add(0, 4 * held, side, 1)

            def edge(pair, carry):
                seen = jnp.concatenate([places[...]] * (SIDE // HD), axis=1)
                seen = seen <= last_row + (token - pair * 2 * UNIT)
                add(pair * 2 * held, 2 * held, side, 1, seen)
                return carry

            lax.fori_loop(whole // 4 * 2, (some + 1) // 2, edge, 0)
            return carry

        full = first_token + low * 512 + window_lag + 1 >= TOKENS

        @pl.when(full)
        def _():
            add(0, UNITS * held, 0, 2)

        @pl.when(jnp.logical_not(full))
        def _():
            lax.fori_loop(0, 2, one_side, 0)

        if not last:
            return carry

        total = jnp.concatenate([norm[block * 2], norm[block * 2 + 1]], axis=1)
        total = jnp.sum(total, axis=0, keepdims=True)
        in_range = jnp.where((total >= SUM_LOW) & (total <= SUM_HIGH), 1.0, 0.0)
        fine = jnp.min(in_range) > 0.5

        def give(mixed, total):
            attended = (mixed / total).T.astype(jnp.bfloat16)
            for index, (pair, head) in enumerate(pairs):
                rows = attended[index * ROWS : (index + 1) * ROWS]
                out_ref[sources[pair], :, head * HD : (head + 1) * HD] = rows

        @pl.when(fine)
        def _():
            give(jnp.concatenate([acc[block * 2], acc[block * 2 + 1]], axis=1), total)

        @pl.when(jnp.logical_not(fine))
        def _():
            for index, piece in enumerate(earlier + pieces[:2]):
                pltpu.sync_copy(piece, spare.at[index])
            for swap in range(2):
                pltpu.sync_copy(pieces[2 + swap], spare.at[7, swap])
            spare_acc[...] = jnp.zeros_like(spare_acc)
            source_x = [low * 512 + last_row, (3 - low) * 512 + last_row]
            last_key = first_token + jnp.concatenate(source_x, axis=1)

            def careful(index, carry):
                peak, total = carry
                piece_z, piece_core = jnp.int32(0), jnp.int32(0)
                for slot, (slot_z, slot_core) in enumerate(origins(place)):
                    piece_z = jnp.where(index // 2 == slot, slot_z, piece_z)
                    piece_core = jnp.where(index // 2 == slot, slot_core, piece_core)
                run = spare[index // 2, index % 2].reshape(4 * RUN, 2 * HD)
                scores = dot(run[:, :HD], query[...], NT) * SCALE
                token = lax.broadcasted_iota(jnp.int32, (4 * RUN, HD), 0)
                token = token // (2 * RUN) * 4096 + token // ROWS % 8 * 256 + token % ROWS
                token = token + (piece_core ^ (index % 2)) * 2048 + piece_z * ROWS
                seen = jnp.concatenate([token] * (BLOCK // HD), axis=1) <= last_key
                scores = jnp.where(seen, scores, NEG_BIG)
                new_peak = jnp.maximum(peak, jnp.max(scores, axis=0, keepdims=True))
                factor = jnp.exp2(peak - new_peak)
                weights = jnp.where(seen, jnp.exp2(scores - new_peak), 0.0)
                mixed = dot(run[:, HD:].T, weights.astype(jnp.bfloat16), NN)
                spare_acc[...] = spare_acc[...] * factor + mixed
                return new_peak, total * factor + jnp.sum(weights, axis=0, keepdims=True)

            start = (jnp.full((1, BLOCK), NEG_BIG), jnp.zeros((1, BLOCK)))
            _, total = lax.fori_loop(0, 16, careful, start)
            give(spare_acc[...], total)

        return carry

    lax.fori_loop(0, BLOCKS, one_block, 0)


ACC = jax.ShapeDtypeStruct((2 * BLOCKS, HD, SIDE), jnp.float32)
NORM = jax.ShapeDtypeStruct((2 * BLOCKS, 8, SIDE), jnp.float32)
OUT = jax.ShapeDtypeStruct((MEMBERS, ROWS, HEADS * HD), jnp.bfloat16)


def attend(phase, place, pieces, state, earlier=()):
    smem = pl.BlockSpec(memory_space=pltpu.SMEM)
    vmem = pl.BlockSpec(memory_space=pltpu.VMEM)
    in_specs = [smem] + [vmem] * (len(pieces) + len(state))
    in_specs += [pl.BlockSpec(memory_space=pl.ANY)] * len(earlier)
    total_keys = UNITS * SLOTS[phase] * RUN
    scratch = [
        pltpu.VMEM((total_keys, HD), jnp.bfloat16),
        pltpu.VMEM((HD, total_keys), jnp.bfloat16),
        pltpu.VMEM((2 * SLOTS[phase] * RUN, HD), jnp.int32),
        pltpu.VMEM((BLOCK, HD), jnp.bfloat16),
    ]
    if phase == 2:
        scratch += [
            pltpu.VMEM((8, 2, 16, ROWS, 2 * HD), jnp.bfloat16),
            pltpu.VMEM((HD, BLOCK), jnp.float32),
        ]
    out_shape = ((ACC, NORM), (ACC, NORM), OUT)[phase]
    aliases = {len(pieces) + 2: 0, len(pieces) + 3: 1} if phase == 1 else {}
    return pl.pallas_call(
        functools.partial(attend_kernel, phase),
        out_shape=out_shape,
        in_specs=in_specs,
        out_specs=jax.tree.map(lambda _: vmem, out_shape),
        scratch_shapes=scratch,
        input_output_aliases=aliases,
        compiler_params=pltpu.CompilerParams(vmem_limit_bytes=44 * 2**20),
        cost_estimate=pl.CostEstimate(
            flops=8 * BLOCKS * BLOCK * total_keys * HD,
            bytes_accessed=2**20,
            transcendentals=BLOCKS * BLOCK * total_keys,
        ),
    )(place, *pieces, *state, *earlier)


def pack_kernel(keys_ref, values_ref, out_ref):
    for chip in range(16):
        group = chip // 4 % 2 * 4 + chip % 2 * 2 + chip // 8
        columns = slice(group * HD, (group + 1) * HD)
        out_ref[chip, :, :HD] = keys_ref[:, columns]
        out_ref[chip, :, HD:] = values_ref[:, columns]


X_GROUPS = ((0, 3), (1, 2))
PAIR_MEMBERS = [[x * 8 + i for x in pair for i in range(8)] for pair in X_GROUPS]


def body(queries, keys, values, window_lag):
    x, z, core = (lax.axis_index(name) for name in ("x", "z", "core"))
    kv = pl.pallas_call(
        pack_kernel,
        out_shape=jax.ShapeDtypeStruct((16, ROWS, 2 * HD), jnp.bfloat16),
    )(keys, values)
    held = lax.all_to_all(
        kv, ("y_lo", "x", "y_hi"), split_axis=0, concat_axis=0, tiled=True
    )
    regroup = functools.partial(
        lax.all_to_all,
        axis_name=("x", "y_hi", "y_lo", "core"),
        split_axis=0,
        concat_axis=0,
        tiled=True,
        axis_index_groups=PAIR_MEMBERS,
    )
    by_member = queries.reshape(ROWS, MEMBERS, HEADS * HD).transpose(1, 0, 2)
    by_member, held = lax.optimization_barrier((by_member, held))
    moved = regroup(by_member)

    def other_core(piece):
        return lax.ppermute(piece, "core", [(0, 1), (1, 0)])

    def onward(piece):
        up = [(i * 2, (i + 1) % 8 * 2) for i in range(8)]
        down = [(i * 2 + 1, (i - 1) % 8 * 2 + 1) for i in range(8)]
        return lax.ppermute(piece, ("z", "core"), up + down)

    def both(piece):
        return [piece, other_core(piece)]

    place = jnp.concatenate([jnp.stack([x, z, core]).astype(jnp.int32), window_lag])
    chip = jnp.stack(both(held))
    came1 = onward(chip)
    came2 = onward(came1)
    came2, moved = lax.optimization_barrier((came2, moved))
    came3 = onward(came2)
    near, middle = [chip, *both(came1)], both(came2)
    acc, norm = attend(0, place, near, (moved,))
    came3, acc = lax.optimization_barrier((came3, acc))
    opposite = onward(came3[0])
    far = both(came3)
    acc, norm = attend(1, place, middle, (moved, acc, norm))
    opposite, acc = lax.optimization_barrier((opposite, acc))
    far += both(opposite)
    attended = attend(2, place, far, (moved, acc, norm), near + middle)
    returned = regroup(attended)
    return returned.transpose(1, 0, 2).reshape(ROWS, HQ * HD)


def solution(mesh):
    fine = Mesh(mesh.devices.reshape(4, 2, 8, 2, 2), ("x", "y_hi", "z", "y_lo", "core"))
    spec = P(("y_lo", "core", "x", "y_hi", "z"), None)
    return jax.shard_map(
        body, mesh=fine, in_specs=(spec, spec, spec, P()), out_specs=spec, check_vma=False
    )
```

```python
import functools
import math

import jax
import jax.numpy as jnp
from jax import lax
from jax.experimental import pallas as pl
from jax.experimental.pallas import tpu as pltpu
from jax.sharding import Mesh, PartitionSpec as P

HQ = 128
KV = 8
HD = 128
TOKENS = 8192

ROWS = 32
MEMBERS = 16
HEADS = HQ // MEMBERS
BLOCK = 1024
BLOCKS = 4
UNIT = 1024
RUN = 128
UNITS = TOKENS // UNIT
SLOTS = (3, 2, 3)
NEG_BIG = -1e30
SCALE = math.log2(math.e) / math.sqrt(HD)
SUM_LOW = 2.0**-90
SUM_HIGH = 2.0**120

NT = (((1,), (1,)), ((), ()))
NN = (((1,), (0,)), ((), ()))


def dot(a, b, dims):
    return lax.dot_general(a, b, dims, preferred_element_type=jnp.float32)


def origins(place):
    z, core = place[1], place[2]
    toward = core * 2 - 1
    found = [(z, core)]
    for distance in range(1, 4):
        for ring in range(2):
            found.append(((z + 8 + (1 - 2 * ring) * toward * distance) % 8, core ^ ring))
    return found + [((z + 4) % 8, core)]


def attend_kernel(phase, *refs):
    first, last = phase == 0, phase == 2
    slots = SLOTS[phase]
    held = slots * RUN
    count = (3, 2, 4)[phase]
    place, pieces, refs = refs[0], refs[1 : 1 + count], refs[1 + count :]
    if first:
        q_ref, acc, norm, keys, values_t, places, query = refs
    elif not last:
        q_ref, _, _, acc, norm, keys, values_t, places, query = refs
    else:
        (q_ref, acc, norm), earlier, refs = refs[:3], refs[3:8], refs[8:]
        out_ref, keys, values_t, places, query, spare, spare_acc = refs
    x, z, core, window_lag = place[0], place[1], place[2], place[3]
    base = sum(SLOTS[:phase])

    row = lax.broadcasted_iota(jnp.int32, (RUN, HD), 0)
    row = row // ROWS * 256 + row % ROWS
    for slot in range(slots):
        piece_z, piece_core = origins(place)[base + slot]
        tokens = row + piece_z * ROWS
        places[slot * RUN : (slot + 1) * RUN, :] = tokens
        for unit in range(1, 4):
            at = unit * held + slot * RUN
            places[at : at + RUN, :] = tokens + unit * UNIT
        for swap in range(2):
            piece = pieces[slot + swap] if last and slot == 2 else pieces[slot].at[swap]
            for part in range(4):
                unit = part // 2 * 4 + (piece_core ^ swap) * 2 + part % 2
                rows = pl.ds(pl.multiple_of(unit * held + slot * RUN, RUN), RUN)
                run = piece[part * 4 : part * 4 + 4].reshape(RUN, 2 * HD)
                keys[rows, :] = run[:, :HD]
                values_t[:, rows] = run[:, HD:].T

    def one_block(block, carry):
        low = jnp.minimum(x, 3 - x)
        first_token = block * 2048 + z * ROWS
        sources = [pair * 4 + block for pair in range(4)]
        pairs = [(pair, head) for pair in range(4) for head in range(HEADS)]
        for index, (pair, head) in enumerate(pairs):
            part = q_ref[sources[pair], :, head * HD : (head + 1) * HD]
            query[index * ROWS : (index + 1) * ROWS, :] = part
        if first:
            acc[block] = jnp.zeros((HD, BLOCK), jnp.float32)
            norm[block] = jnp.zeros((8, BLOCK), jnp.float32)

        row = lax.broadcasted_iota(jnp.int32, (1, BLOCK), 1)
        source_x = jnp.where(row < BLOCK // 2, low, 3 - low)
        last_key = first_token + window_lag + row % ROWS
        last_key = last_key + source_x * 512 + row // (BLOCK // 4) % 2 * 256
        all_see = jnp.minimum(first_token + low * 512 + window_lag + 1, TOKENS)
        some_see = first_token + (3 - low) * 512 + 256 + ROWS + window_lag
        some_see = jnp.minimum(some_see, TOKENS)
        whole = all_see // UNIT
        some = (some_see + UNIT - 1) // UNIT

        def scores_of(start, size):
            return dot(keys[pl.ds(start, size), :], query[...], NT) * SCALE

        def add(scores, turned):
            weights = jnp.exp2(scores)
            size = scores.shape[0]
            norm[block] += jnp.sum(weights.reshape(size // 8, 8, BLOCK), axis=0)
            acc[block] += dot(turned, weights.astype(jnp.bfloat16), NN)

        def step(unit, units, masked=False):
            start = pl.multiple_of(unit * held, 2 * held)
            size = units * held
            scores = scores_of(start, size)
            if masked:
                seen = jnp.concatenate([places[:size, :]] * (BLOCK // HD), axis=1)
                scores = jnp.where(seen <= last_key - unit * UNIT, scores, NEG_BIG)
            add(scores, values_t[:, pl.ds(start, size)])

        @pl.when(whole == UNITS)
        def _():
            step(0, UNITS)

        @pl.when((whole >= 4) & (whole < UNITS))
        def _():
            step(0, 4)

        def edge(pair, carry):
            step(pair * 2, 2, True)
            return carry

        pair, end = whole // 4 * 2, (some + 1) // 2
        several = end - pair >= 2

        @pl.when(several)
        def _():
            step(pair * 2, 4, True)

        lax.fori_loop(jnp.where(several, pair + 2, pair), end, edge, 0)
        if not last:
            return carry

        total = jnp.sum(norm[block], axis=0, keepdims=True)
        in_range = jnp.where((total >= SUM_LOW) & (total <= SUM_HIGH), 1.0, 0.0)
        fine = jnp.min(in_range) > 0.5

        def give(mixed, total):
            attended = (mixed / total).T.astype(jnp.bfloat16)
            for index, (pair, head) in enumerate(pairs):
                rows = attended[index * ROWS : (index + 1) * ROWS]
                out_ref[sources[pair], :, head * HD : (head + 1) * HD] = rows

        @pl.when(fine)
        def _():
            give(acc[block], total)

        @pl.when(jnp.logical_not(fine))
        def _():
            for index, piece in enumerate(earlier + pieces[:2]):
                pltpu.sync_copy(piece, spare.at[index])
            for swap in range(2):
                pltpu.sync_copy(pieces[2 + swap], spare.at[7, swap])
            spare_acc[...] = jnp.zeros_like(spare_acc)

            def careful(index, carry):
                peak, total = carry
                piece_z, piece_core = jnp.int32(0), jnp.int32(0)
                for slot, (slot_z, slot_core) in enumerate(origins(place)):
                    piece_z = jnp.where(index // 2 == slot, slot_z, piece_z)
                    piece_core = jnp.where(index // 2 == slot, slot_core, piece_core)
                run = spare[index // 2, index % 2].reshape(4 * RUN, 2 * HD)
                scores = dot(run[:, :HD], query[...], NT) * SCALE
                token = lax.broadcasted_iota(jnp.int32, (4 * RUN, HD), 0)
                token = token // (2 * RUN) * 4096 + token // ROWS % 8 * 256 + token % ROWS
                token = token + (piece_core ^ (index % 2)) * 2048 + piece_z * ROWS
                seen = jnp.concatenate([token] * (BLOCK // HD), axis=1) <= last_key
                scores = jnp.where(seen, scores, NEG_BIG)
                new_peak = jnp.maximum(peak, jnp.max(scores, axis=0, keepdims=True))
                factor = jnp.exp2(peak - new_peak)
                weights = jnp.where(seen, jnp.exp2(scores - new_peak), 0.0)
                mixed = dot(run[:, HD:].T, weights.astype(jnp.bfloat16), NN)
                spare_acc[...] = spare_acc[...] * factor + mixed
                return new_peak, total * factor + jnp.sum(weights, axis=0, keepdims=True)

            start = (jnp.full((1, BLOCK), NEG_BIG), jnp.zeros((1, BLOCK)))
            _, total = lax.fori_loop(0, 16, careful, start)
            give(spare_acc[...], total)

        return carry

    lax.fori_loop(0, BLOCKS, one_block, 0)


ACC = jax.ShapeDtypeStruct((BLOCKS, HD, BLOCK), jnp.float32)
NORM = jax.ShapeDtypeStruct((BLOCKS, 8, BLOCK), jnp.float32)
OUT = jax.ShapeDtypeStruct((MEMBERS, ROWS, HEADS * HD), jnp.bfloat16)


def attend(phase, place, pieces, state, earlier=()):
    smem = pl.BlockSpec(memory_space=pltpu.SMEM)
    vmem = pl.BlockSpec(memory_space=pltpu.VMEM)
    in_specs = [smem] + [vmem] * (len(pieces) + len(state))
    in_specs += [pl.BlockSpec(memory_space=pl.ANY)] * len(earlier)
    total_keys = UNITS * SLOTS[phase] * RUN
    scratch = [
        pltpu.VMEM((total_keys, HD), jnp.bfloat16),
        pltpu.VMEM((HD, total_keys), jnp.bfloat16),
        pltpu.VMEM((4 * SLOTS[phase] * RUN, HD), jnp.int32),
        pltpu.VMEM((BLOCK, HD), jnp.bfloat16),
    ]
    if phase == 2:
        scratch += [
            pltpu.VMEM((8, 2, 16, ROWS, 2 * HD), jnp.bfloat16),
            pltpu.VMEM((HD, BLOCK), jnp.float32),
        ]
    out_shape = ((ACC, NORM), (ACC, NORM), OUT)[phase]
    aliases = {len(pieces) + 2: 0, len(pieces) + 3: 1} if phase == 1 else {}
    return pl.pallas_call(
        functools.partial(attend_kernel, phase),
        out_shape=out_shape,
        in_specs=in_specs,
        out_specs=jax.tree.map(lambda _: vmem, out_shape),
        scratch_shapes=scratch,
        input_output_aliases=aliases,
        compiler_params=pltpu.CompilerParams(vmem_limit_bytes=44 * 2**20),
        cost_estimate=pl.CostEstimate(
            flops=8 * BLOCKS * BLOCK * total_keys * HD,
            bytes_accessed=2**20,
            transcendentals=BLOCKS * BLOCK * total_keys,
        ),
    )(place, *pieces, *state, *earlier)


def pack_kernel(keys_ref, values_ref, out_ref):
    for chip in range(16):
        group = chip // 4 % 2 * 4 + chip % 2 * 2 + chip // 8
        columns = slice(group * HD, (group + 1) * HD)
        out_ref[chip, :, :HD] = keys_ref[:, columns]
        out_ref[chip, :, HD:] = values_ref[:, columns]


X_GROUPS = ((0, 3), (1, 2))
PAIR_MEMBERS = [[x * 8 + i for x in pair for i in range(8)] for pair in X_GROUPS]


def body(queries, keys, values, window_lag):
    x, z, core = (lax.axis_index(name) for name in ("x", "z", "core"))
    kv = pl.pallas_call(
        pack_kernel,
        out_shape=jax.ShapeDtypeStruct((16, ROWS, 2 * HD), jnp.bfloat16),
    )(keys, values)
    held = lax.all_to_all(
        kv, ("y_lo", "x", "y_hi"), split_axis=0, concat_axis=0, tiled=True
    )
    regroup = functools.partial(
        lax.all_to_all,
        axis_name=("x", "y_hi", "y_lo", "core"),
        split_axis=0,
        concat_axis=0,
        tiled=True,
        axis_index_groups=PAIR_MEMBERS,
    )
    by_member = queries.reshape(ROWS, MEMBERS, HEADS * HD).transpose(1, 0, 2)
    by_member, held = lax.optimization_barrier((by_member, held))
    moved = regroup(by_member)

    def other_core(piece):
        return lax.ppermute(piece, "core", [(0, 1), (1, 0)])

    def onward(piece):
        up = [(i * 2, (i + 1) % 8 * 2) for i in range(8)]
        down = [(i * 2 + 1, (i - 1) % 8 * 2 + 1) for i in range(8)]
        return lax.ppermute(piece, ("z", "core"), up + down)

    def both(piece):
        return [piece, other_core(piece)]

    place = jnp.concatenate([jnp.stack([x, z, core]).astype(jnp.int32), window_lag])
    chip = jnp.stack(both(held))
    came1 = onward(chip)
    came2 = onward(came1)
    came2, moved = lax.optimization_barrier((came2, moved))
    came3 = onward(came2)
    near, middle = [chip, *both(came1)], both(came2)
    acc, norm = attend(0, place, near, (moved,))
    came3, acc = lax.optimization_barrier((came3, acc))
    opposite = onward(came3[0])
    far = both(came3)
    acc, norm = attend(1, place, middle, (moved, acc, norm))
    opposite, acc = lax.optimization_barrier((opposite, acc))
    far += both(opposite)
    attended = attend(2, place, far, (moved, acc, norm), near + middle)
    returned = regroup(attended)
    return returned.transpose(1, 0, 2).reshape(ROWS, HQ * HD)


def solution(mesh):
    fine = Mesh(mesh.devices.reshape(4, 2, 8, 2, 2), ("x", "y_hi", "z", "y_lo", "core"))
    spec = P(("y_lo", "core", "x", "y_hi", "z"), None)
    return jax.shard_map(
        body, mesh=fine, in_specs=(spec, spec, spec, P()), out_specs=spec, check_vma=False
    )
```
